32 devices in a mesh: dp: 4 (over y, core), tensor: 8 (over z, x).
Axes of the slice: x: 2, y: 2, z: 4, core: 2. Of those that a mesh axis runs over, the one named last changes fastest.
Arguments:
- tokens: bfloat16 [16384, 3072], P(('dp', 'tensor')), parts along dimension 0, may hold values from -6 to 6
- expert_ids: int32 [16384, 4], P(('dp', 'tensor')), parts along dimension 0, may hold values from 0 to 15, as said below
- gate_probs: float32 [16384, 4], P(('dp', 'tensor')), parts along dimension 0, may hold values from 0.1 to 1
- gate_weight: bfloat16 [3072, 5376], P(None, 'tensor'), may hold values from -0.109375 to 0.109375
- up_weight: bfloat16 [3072, 5376], P(None, 'tensor'), may hold values from -0.109375 to 0.109375
- down_weight: bfloat16 [5376, 3072], P('tensor'), may hold values from -0.078125 to 0.078125
Outputs:
- mixed: bfloat16 [16384, 3072], P(('dp', 'tensor')), parts along dimension 0
The draws below stay inside these ranges and needn't reach their ends.
There are 4 independent parts, one for each index of `dp`. The reference program is written for one: setup_inputs(seed, part) draws one part's arguments, and reference() takes and returns one part's arrays. A program takes and returns all parts, laid end to end along the dimension named above; an argument that names none is the same for every part. Nothing has to cross between parts.
Inputs may be any that keep to these rules, and one draw needn't show every extreme that they name: `expert_ids`: each row names 4 different experts. In each block of 128 consecutive tokens (rows b * 128 to (b + 1) * 128 - 1) between 1 and 32 rows name expert 0, and some block has exactly 32.
All inputs are finite; a program needn't handle non-finite values.
Results may differ from the reference program's by a relative error of at most 0.019.
Values may be sent and summed in bfloat16 or wider, within the bound.
A program may use at most 128 MiB of HBM per device.

```python
import jax
import jax.numpy as jnp
from jax import lax

D = 3072
FF = 5376
EXPERTS = 16
TOP = 4
CT = 128
CAP = 32
TOKENS = 4096
N_TENSOR = 8


def draw_expert_ids(key, part):
    key = jax.random.fold_in(key, 11)
    key_list = jax.random.split(key, 5)
    block_count = TOKENS // CT
    counts = jax.random.randint(key_list[0], (block_count,), 1, CAP + 1)
    forced = jax.random.randint(key_list[1], (), 0, block_count)
    counts = jnp.where(jnp.arange(block_count) == forced, CAP, counts)
    scores = jax.random.randint(key_list[2], (block_count, CT), 0, 1 << 20) * CT + jnp.arange(CT)[None, :]
    rank_order = jnp.argsort(jnp.argsort(scores, axis=1), axis=1)
    routed = (rank_order < counts[:, None]).reshape(TOKENS)
    others = jax.random.randint(key_list[3], (TOKENS, EXPERTS - 1), 0, 1 << 20) * EXPERTS + jnp.arange(EXPERTS - 1)[None, :]
    chosen = jnp.argsort(others, axis=1)[:, :TOP] + 1
    position = jax.random.randint(key_list[4], (TOKENS,), 0, TOP)
    window = routed[:, None] & (jnp.arange(TOP)[None, :] == position[:, None])
    return jnp.where(window, 0, chosen).astype(jnp.int32)


def shard_levels(own_key, shape, pieces, low, top_value):
    gain, own = 1.0, jax.random.fold_in(own_key, 6)
    for dim, parts in pieces:
        draws = jnp.exp(jax.random.uniform(jax.random.fold_in(own, dim), (parts,), jnp.float32, low / len(pieces), top_value / len(pieces)))
        gain = gain * jnp.repeat(draws, shape[dim] // parts).reshape([-1 if axis == dim else 1 for axis in range(len(shape))])
    return gain


def scatter_about(rng, shape, width, bound, cuts=(), kind=jnp.bfloat16):
    values = width * jax.random.normal(rng, shape, jnp.float32)
    if cuts:
        values = values * shard_levels(rng, shape, cuts, -0.22, 0.18)
    return jnp.clip(values, -bound, bound).astype(kind)


def setup_inputs(seed: int = 0, part: int = 0) -> dict:
    streams_of = jax.random.split(jax.random.key(seed), 7)
    part_splits = jax.random.split(jax.random.fold_in(streams_of[6], part), 7)
    tokens = scatter_about(part_splits[0], (TOKENS, D), 1.0, 6.0, ((0, 8),))
    expert_ids = draw_expert_ids(jax.random.fold_in(jax.random.fold_in(streams_of[6], part), 71), part)
    gate_probs = jnp.clip(0.1 + 0.9 * jax.random.uniform(part_splits[2], (TOKENS, TOP), jnp.float32) ** shard_levels(part_splits[2], (TOKENS, TOP), ((0, 8),), -0.2, 0.2), 0.1, 1.0)
    gate_weight = scatter_about(streams_of[3], (D, FF), D ** -0.5, 0.109375, ((1, 8),))
    up_weight = scatter_about(streams_of[4], (D, FF), D ** -0.5, 0.109375, ((1, 8),))
    down_weight = scatter_about(streams_of[5], (FF, D), FF ** -0.5, 0.078125, ((0, 8),))
    return dict(tokens=tokens, expert_ids=expert_ids, gate_probs=gate_probs, gate_weight=gate_weight, up_weight=up_weight, down_weight=down_weight)


def reference(tokens, expert_ids, gate_probs, gate_weight, up_weight, down_weight):
    is_window = expert_ids == 0
    routed = jnp.any(is_window, axis=1)
    gate_share = jnp.sum(jnp.where(is_window, gate_probs, 0.0), axis=1)
    block_count = TOKENS // CT
    routed_blocks = routed.reshape(block_count, CT)
    slot_place = jnp.cumsum(routed_blocks.astype(jnp.int32), axis=1).astype(jnp.int32) - 1
    selector = (slot_place[:, None, :] == jnp.arange(CAP, dtype=jnp.int32)[None, :, None]) & routed_blocks[:, None, :]
    slot_rows = jnp.einsum("bst,btd->bsd", selector.astype(jnp.float32), tokens.reshape(block_count, CT, D).astype(jnp.float32))
    slot_rows = slot_rows.astype(jnp.bfloat16).reshape(block_count * CAP, D)
    gate_pre = jnp.dot(slot_rows, gate_weight, preferred_element_type=jnp.float32)
    up_pre = jnp.dot(slot_rows, up_weight, preferred_element_type=jnp.float32)
    hidden = (jax.nn.silu(gate_pre) * up_pre).astype(jnp.bfloat16)
    unit_width = FF // N_TENSOR

    def add_part(part_index, running_sum):
        start_unit = jnp.asarray(part_index).astype(jnp.int32) * unit_width
        columns = lax.dynamic_slice_in_dim(hidden, start_unit, unit_width, 1)
        down_rows = lax.dynamic_slice_in_dim(down_weight, start_unit, unit_width, 0)
        partial_sum = jnp.dot(columns, down_rows, preferred_element_type=jnp.float32).astype(jnp.bfloat16)
        partial_sum = lax.optimization_barrier(partial_sum)
        return running_sum + partial_sum.astype(jnp.float32)

    expert_out = lax.fori_loop(0, N_TENSOR, add_part, jnp.zeros((block_count * CAP, D), jnp.float32))
    slot_index = jnp.where(routed_blocks, jnp.arange(block_count, dtype=jnp.int32)[:, None] * CAP + slot_place, 0)
    picked = jnp.take(expert_out, slot_index.reshape(TOKENS).astype(jnp.int32), axis=0)
    mixed = jnp.where(routed[:, None], gate_share[:, None] * picked, 0.0)
    return mixed.astype(jnp.bfloat16)
```

```python
import functools

import jax
import jax.numpy as jnp
from jax import lax
from jax.experimental import pallas as pl
from jax.experimental.pallas import tpu as pltpu
from jax.sharding import PartitionSpec as P

CT = 128
CAP = 32
ROWS_Z = 4
MESH = pl.DeviceIdType.MESH


def expert_kernel(
    zs, xs, ra, wide,
    slot_ref, gw_hbm, uw_hbm, dw_hbm, out_ref,
    g, p, rz, rxa, rxb, h, gw, uw, dw,
    wsem, agz_s, agz_r, axa_s, axa_r, axb_s, axb_r,
    rz_s, rz_r, rxa_s, rxa_r, rxb_s, rxb_r,
):
    rows, width = slot_ref.shape
    rb = rows - ra
    hidden = gw.shape[1]
    me = lax.axis_index("tensor")
    dp = lax.axis_index("dp")
    z = me // xs
    x = me % xs

    def dev(zz, xx):
        return (dp, zz * xs + xx)

    def a_rows(sx):
        return pl.ds(pl.multiple_of(sx * rows, 16), ra)

    def b_rows(sx):
        return pl.ds(pl.multiple_of(sx * rows + ra, 16), rb)

    def other(k):
        return (x + k) % xs

    def source(k):
        return (x + xs - k) % xs

    def unit_rows(unit):
        return a_rows(x) if unit is None else b_rows(unit)

    def unit_sem(unit):
        return 0 if unit is None else 1 + unit

    def slot_rows(unit):
        if unit is None:
            return pl.ds(0, ra)
        return pl.ds(pl.multiple_of(ra + unit * rb, 16), rb)

    units = [None] + list(range(xs))

    def copy(src, dst, s, r, to):
        return pltpu.make_async_remote_copy(
            src_ref=src, dst_ref=dst, send_sem=s, recv_sem=r,
            device_id=to, device_id_type=MESH,
        )

    def gather_z(d, s, unit):
        part = g.at[s, unit_rows(unit)]
        i = unit_sem(unit)
        return copy(part, part, agz_s.at[d, s, i], agz_r.at[s, i], dev(z + 2 * d - 1, x))

    def gather_xa(k, s, sx):
        part = g.at[s, a_rows(sx)]
        return copy(part, part, axa_s.at[s, k - 1], axa_r.at[s, k - 1], dev(z, other(k)))

    def gather_xb(k, sx):
        part = g.at[z, b_rows(sx)]
        return copy(part, part, axb_s.at[k - 1], axb_r.at[k - 1], dev(z, other(k)))

    def reduce_xa(k, s):
        return copy(
            p.at[s, a_rows(other(k))], rxa.at[k - 1, s],
            rxa_s.at[s, k - 1], rxa_r.at[s, k - 1], dev(z, other(k)),
        )

    def reduce_xb(k):
        return copy(
            p.at[z, b_rows(other(k))], rxb.at[k - 1],
            rxb_s.at[k - 1], rxb_r.at[k - 1], dev(z, other(k)),
        )

    def reduce_z(d, o, unit):
        i = unit_sem(unit)
        return copy(
            p.at[o, unit_rows(unit)], rz.at[d, o, slot_rows(unit)],
            rz_s.at[d, o, i], rz_r.at[d, o, i], dev(z + 2 * d - 1, x),
        )

    def has_next(d):
        return z < zs - 1 if d == 1 else z > 0

    weights = [
        pltpu.make_async_copy(a, b, wsem.at[i])
        for i, (a, b) in enumerate(((gw_hbm, gw), (uw_hbm, uw), (dw_hbm, dw)))
    ]
    for w in weights:
        w.start()

    barrier = pltpu.get_barrier_semaphore()
    for d in (0, 1):
        @pl.when(has_next(d))
        def _():
            pl.semaphore_signal(barrier, inc=1, device_id=dev(z + 2 * d - 1, x), device_id_type=MESH)
    for k in range(1, xs):
        pl.semaphore_signal(barrier, inc=1, device_id=dev(z, other(k)), device_id_type=MESH)
    g[z, pl.ds(pl.multiple_of(x * rows, 16), rows), :] = slot_ref[...]
    ends = (z == 0).astype(jnp.int32) + (z == zs - 1).astype(jnp.int32)
    pl.semaphore_wait(barrier, xs + 1 - ends)

    for k in range(1, xs):
        gather_xb(k, x).start()
    for d in (0, 1):
        @pl.when(has_next(d))
        def _():
            gather_z(d, z, None).start()
            gather_z(d, z, x).start()
    for k in range(1, xs):
        gather_xa(k, z, x).start()

    @pl.when(z == zs - 1)
    def _():
        rz[0] = jnp.zeros(rz.shape[1:], rz.dtype)

    @pl.when(z == 0)
    def _():
        rz[1] = jnp.zeros(rz.shape[1:], rz.dtype)

    for k in range(1, xs):
        gather_xb(k, source(k)).wait_recv()
        for d in (0, 1):
            @pl.when(has_next(d))
            def _():
                gather_z(d, z, source(k)).start()

    def compute(s):
        for k in range(1, xs):
            gather_xa(k, s, source(k)).wait_recv()
        for c in range(0, hidden, 256):
            n = min(256, hidden - c)
            lhs = g[s]
            gate = jnp.dot(lhs, gw[:, c:c + n], preferred_element_type=jnp.float32)
            up = jnp.dot(lhs, uw[:, c:c + n], preferred_element_type=jnp.float32)
            h[:, c:c + n] = (gate / (1.0 + jnp.exp(-gate)) * up).astype(h.dtype)

        def columns(i, carry):
            at = pl.ds(pl.multiple_of(i * wide, 128), wide)
            p[s, :, at] = jnp.dot(
                h[...], dw[:, at], preferred_element_type=jnp.float32
            ).astype(p.dtype)
            return carry

        lax.fori_loop(0, width // wide, columns, 0)
        for k in range(1, xs):
            reduce_xa(k, s).start()

    for w in weights:
        w.wait()
    compute(z)

    def add_rows(count, target, parts):
        def body(i, carry):
            i = pl.multiple_of(i * 16, 16)
            total = None
            for part in parts:
                value = part(pl.ds(i, 16)).astype(jnp.float32)
                total = value if total is None else total + value
            target(i, total)
            return carry

        lax.fori_loop(0, count // 16, body, 0)

    def p_part(o, unit):
        base = x * rows if unit is None else unit * rows + ra

        def read(at):
            return p[o, pl.ds(pl.multiple_of(base + at.start, 16), 16), :]

        def write(i, value):
            p[o, pl.ds(pl.multiple_of(base + i, 16), 16), :] = value.astype(p.dtype)

        return read, write

    def rz_part(d, o, unit):
        base = 0 if unit is None else ra + unit * rb

        def read(at):
            return rz[d, o, pl.ds(pl.multiple_of(base + at.start, 16), 16), :]

        return read

    def rxa_parts(o):
        return [lambda at, k=k: rxa[k - 1, o, at, :] for k in range(1, xs)]

    def step(t, carry):
        for d in (0, 1):
            s = z - t if d == 1 else z + t

            @pl.when((s >= 0) & (s < zs))
            def _():
                for unit in units:
                    gather_z(d, s, unit).wait_recv()

                    @pl.when(has_next(d))
                    def _():
                        gather_z(d, s, unit).start()
                    if unit is None:
                        for k in range(1, xs):
                            gather_xa(k, s, x).start()

        def slab(j, c):
            s = z + t * (1 - 2 * j)

            @pl.when((s >= 0) & (s < zs))
            def _():
                compute(s)
            return c

        lax.fori_loop(0, 2, slab, 0)

        for unit in units:
            def flow(j, c):
                d = jnp.where(z < zs // 2, 1 - j, j)
                o = jnp.where(d == 0, zs - 1 - t, t)
                dist = jnp.where(d == 0, z - o, o - z)
                fed = jnp.where(d == 0, zs - 1 - z, z)

                @pl.when(dist > 0)
                def _():
                    parts = []
                    if unit is None:
                        for k in range(1, xs):
                            reduce_xa(k, o).wait_recv()
                        parts = rxa_parts(o)

                    @pl.when(fed > 0)
                    def _():
                        reduce_z(d, o, unit).wait_recv()
                    read, write = p_part(o, unit)
                    add_rows(ra if unit is None else rb, write, [read, rz_part(d, o, unit)] + parts)
                    reduce_z(d, o, unit).start()
                return c

            lax.fori_loop(0, 2, flow, 0)
        return carry

    lax.fori_loop(1, zs, step, 0)

    def take(unit):
        for d in (0, 1):
            @pl.when(has_next(1 - d))
            def _():
                reduce_z(d, z, unit).wait_recv()

    for k in range(1, xs):
        take(other(k))
        read, write = p_part(z, other(k))
        add_rows(rb, write, [read, rz_part(0, z, other(k)), rz_part(1, z, other(k))])
        reduce_xb(k).start()

    def out_at(base):
        def write(i, value):
            out_ref[pl.ds(pl.multiple_of(base + i, 16), 16), :] = value.astype(out_ref.dtype)
        return write

    take(None)
    for k in range(1, xs):
        reduce_xa(k, z).wait_recv()
    add_rows(
        ra, out_at(0),
        [p_part(z, None)[0], rz_part(0, z, None), rz_part(1, z, None)] + rxa_parts(z),
    )
    take(x)
    for k in range(1, xs):
        reduce_xb(k).wait_recv()
    add_rows(
        rb, out_at(ra),
        [p_part(z, x)[0], rz_part(0, z, x), rz_part(1, z, x)]
        + [lambda at, k=k: rxb[k - 1, at, :] for k in range(1, xs)],
    )

    for k in range(1, xs):
        gather_xb(k, x).wait_send()
        reduce_xb(k).wait_send()

    def sent(s, carry):
        for k in range(1, xs):
            gather_xa(k, s, x).wait_send()
            reduce_xa(k, s).wait_send()
        for d in (0, 1):
            behind = s <= z if d == 1 else s >= z
            ahead = s > z if d == 1 else s < z

            @pl.when(has_next(d) & behind)
            def _():
                for unit in units:
                    gather_z(d, s, unit).wait_send()

            @pl.when(ahead)
            def _():
                for unit in units:
                    reduce_z(d, s, unit).wait_send()
        return carry

    lax.fori_loop(0, zs, sent, 0)


def expert_sum(slot_rows, gate_weight, up_weight, down_weight, tensor):
    rows, width = slot_rows.shape
    hidden = gate_weight.shape[1]
    zs = ROWS_Z if tensor % ROWS_Z == 0 else 1
    xs = tensor // zs
    ra = rows * 5 // 8 // 16 * 16
    rb = rows - ra
    wide = 512 if width % 512 == 0 else 128
    dt = slot_rows.dtype
    dma = pltpu.SemaphoreType.DMA
    flops = 6 * rows * tensor * width * hidden
    return pl.pallas_call(
        functools.partial(expert_kernel, zs, xs, ra, wide),
        out_shape=jax.ShapeDtypeStruct((rows, width), dt),
        in_specs=[pl.BlockSpec(memory_space=pltpu.VMEM)]
        + [pl.BlockSpec(memory_space=pl.ANY)] * 3,
        out_specs=pl.BlockSpec(memory_space=pltpu.VMEM),
        scratch_shapes=[
            pltpu.VMEM((zs, xs * rows, width), dt),
            pltpu.VMEM((zs, xs * rows, width), dt),
            pltpu.VMEM((2, zs, ra + xs * rb, width), dt),
            pltpu.VMEM((xs - 1, zs, ra, width), dt),
            pltpu.VMEM((xs - 1, rb, width), dt),
            pltpu.VMEM((xs * rows, hidden), dt),
            pltpu.VMEM(gate_weight.shape, dt),
            pltpu.VMEM(up_weight.shape, dt),
            pltpu.VMEM(down_weight.shape, dt),
            dma((3,)),
            dma((2, zs, xs + 1)), dma((zs, xs + 1)),
            dma((zs, xs - 1)), dma((zs, xs - 1)),
            dma((xs - 1,)), dma((xs - 1,)),
            dma((2, zs, xs + 1)), dma((2, zs, xs + 1)),
            dma((zs, xs - 1)), dma((zs, xs - 1)),
            dma((xs - 1,)), dma((xs - 1,)),
        ],
        compiler_params=pltpu.CompilerParams(
            collective_id=0, has_side_effects=True, vmem_limit_bytes=60 * 2**20
        ),
        cost_estimate=pl.CostEstimate(
            flops=flops, bytes_accessed=6 * width * hidden + 4 * rows * width,
            transcendentals=rows * tensor * hidden,
        ),
    )(slot_rows, gate_weight, up_weight, down_weight)


def on_device(tensor, tokens, expert_ids, gate_probs, gate_weight, up_weight, down_weight):
    count, width = tokens.shape
    spans = count // CT
    is_window = expert_ids == 0
    routed = jnp.any(is_window, axis=1)
    gate_share = jnp.sum(jnp.where(is_window, gate_probs, 0.0), axis=1)
    routed_blocks = routed.reshape(spans, CT)
    slot_place = jnp.cumsum(routed_blocks.astype(jnp.int32), axis=1) - 1
    selector = (
        (slot_place[:, None, :] == jnp.arange(CAP, dtype=jnp.int32)[None, :, None])
        & routed_blocks[:, None, :]
    ).astype(jnp.bfloat16)
    slot_rows = jnp.einsum(
        "bst,btd->bsd", selector, tokens.reshape(spans, CT, width),
        preferred_element_type=jnp.float32,
    ).astype(jnp.bfloat16)
    expert_out = expert_sum(
        slot_rows.reshape(spans * CAP, width), gate_weight, up_weight, down_weight, tensor
    )
    picked = jnp.einsum(
        "bst,bsd->btd", selector, expert_out.reshape(spans, CAP, width),
        preferred_element_type=jnp.float32,
    )
    mixed = gate_share.reshape(spans, CT)[:, :, None] * picked
    return mixed.astype(jnp.bfloat16).reshape(count, width)


def solution(mesh):
    in_specs = (
        P(("dp", "tensor"), None),
        P(("dp", "tensor"), None),
        P(("dp", "tensor"), None),
        P(None, "tensor"),
        P(None, "tensor"),
        P("tensor", None),
    )
    out_specs = P(("dp", "tensor"), None)
    return jax.shard_map(
        functools.partial(on_device, mesh.shape["tensor"]),
        mesh=mesh, in_specs=in_specs, out_specs=out_specs, check_vma=False,
    )
```

```python
import functools

import jax
import jax.numpy as jnp
from jax import lax
from jax.experimental import pallas as pl
from jax.experimental.pallas import tpu as pltpu
from jax.sharding import PartitionSpec as P

CT = 128
CAP = 32
ROWS_Z = 4
PIECE = 32
MESH = pl.DeviceIdType.MESH


def cuts(rows):
    return [(at, min(PIECE, rows - at)) for at in range(0, rows, PIECE)]


def dot_t(a, b):
    return lax.dot_general(
        a, b, (((1,), (1,)), ((), ())), preferred_element_type=jnp.float32
    )


def expert_kernel(
    zs, xs, ra, wide,
    slot_ref, gw_hbm, uw_hbm, dw_hbm, out_ref,
    g, p, rz, rxa, rxb, h, gw, uw, dw,
    wsem, agz_s, agz_r, axa_s, axa_r, axb_s, axb_r,
    rz_s, rz_r, rxa_s, rxa_r, rxb_s, rxb_r,
):
    rows, width = slot_ref.shape
    rb = rows - ra
    hidden = gw.shape[0]
    me = lax.axis_index("tensor")
    dp = lax.axis_index("dp")
    z = me // xs
    x = me % xs

    def dev(zz, xx):
        return (dp, zz * xs + xx)

    def a_rows(sx):
        return pl.ds(pl.multiple_of(sx * rows, 16), ra)

    def b_rows(sx):
        return pl.ds(pl.multiple_of(sx * rows + ra, 16), rb)

    def other(k):
        return (x + k) % xs

    def source(k):
        return (x + xs - k) % xs

    def unit_rows(unit):
        return a_rows(x) if unit is None else b_rows(unit)

    def unit_sem(unit):
        return 0 if unit is None else 1 + unit

    a_cuts = cuts(ra)
    b_cuts = cuts(rb)

    def a_pieces():
        return [(None, at, n, i) for i, (at, n) in enumerate(a_cuts)]

    def b_pieces(sx):
        return [
            (sx, at, n, len(a_cuts) + sx * len(b_cuts) + i)
            for i, (at, n) in enumerate(b_cuts)
        ]

    def p_base(piece):
        sx, at = piece[:2]
        return x * rows + at if sx is None else sx * rows + ra + at

    def rz_base(piece):
        sx, at = piece[:2]
        return at if sx is None else ra + sx * rb + at

    units = [None] + list(range(xs))

    def copy(src, dst, s, r, to):
        return pltpu.make_async_remote_copy(
            src_ref=src, dst_ref=dst, send_sem=s, recv_sem=r,
            device_id=to, device_id_type=MESH,
        )

    def gather_z(d, s, unit):
        part = g.at[s, unit_rows(unit)]
        i = unit_sem(unit)
        return copy(part, part, agz_s.at[d, s, i], agz_r.at[s, i], dev(z + 2 * d - 1, x))

    def gather_xa(k, s, sx):
        part = g.at[s, a_rows(sx)]
        return copy(part, part, axa_s.at[s, k - 1], axa_r.at[s, k - 1], dev(z, other(k)))

    def gather_xb(k, sx):
        part = g.at[z, b_rows(sx)]
        return copy(part, part, axb_s.at[k - 1], axb_r.at[k - 1], dev(z, other(k)))

    def reduce_xa(k, s):
        return copy(
            p.at[s, a_rows(other(k))], rxa.at[k - 1, s],
            rxa_s.at[s, k - 1], rxa_r.at[s, k - 1], dev(z, other(k)),
        )

    def reduce_xb(k):
        return copy(
            p.at[z, b_rows(other(k))], rxb.at[k - 1],
            rxb_s.at[k - 1], rxb_r.at[k - 1], dev(z, other(k)),
        )

    def reduce_z(d, o, piece):
        n, i = piece[2:]
        return copy(
            p.at[o, pl.ds(pl.multiple_of(p_base(piece), 16), n)],
            rz.at[d, o, pl.ds(pl.multiple_of(rz_base(piece), 16), n)],
            rz_s.at[d, o, i], rz_r.at[d, o, i], dev(z + 2 * d - 1, x),
        )

    def has_next(d):
        return z < zs - 1 if d == 1 else z > 0

    weights = [
        pltpu.make_async_copy(a, b, wsem.at[i])
        for i, (a, b) in enumerate(((gw_hbm, gw), (uw_hbm, uw), (dw_hbm, dw)))
    ]
    for w in weights:
        w.start()

    barrier = pltpu.get_barrier_semaphore()
    for d in (0, 1):
        @pl.when(has_next(d))
        def _():
            pl.semaphore_signal(barrier, inc=1, device_id=dev(z + 2 * d - 1, x), device_id_type=MESH)
    for k in range(1, xs):
        pl.semaphore_signal(barrier, inc=1, device_id=dev(z, other(k)), device_id_type=MESH)
    g[z, pl.ds(pl.multiple_of(x * rows, 16), rows), :] = slot_ref[...]
    ends = (z == 0).astype(jnp.int32) + (z == zs - 1).astype(jnp.int32)
    pl.semaphore_wait(barrier, xs + 1 - ends)

    for k in range(1, xs):
        gather_xb(k, x).start()
    for d in (0, 1):
        @pl.when(has_next(d))
        def _():
            gather_z(d, z, None).start()
            gather_z(d, z, x).start()
    for k in range(1, xs):
        gather_xa(k, z, x).start()

    @pl.when(z == zs - 1)
    def _():
        rz[0] = jnp.zeros(rz.shape[1:], rz.dtype)

    @pl.when(z == 0)
    def _():
        rz[1] = jnp.zeros(rz.shape[1:], rz.dtype)

    for k in range(1, xs):
        gather_xb(k, source(k)).wait_recv()
        for d in (0, 1):
            @pl.when(has_next(d))
            def _():
                gather_z(d, z, source(k)).start()

    def compute(s):
        for k in range(1, xs):
            gather_xa(k, s, source(k)).wait_recv()
        for c in range(0, hidden, 256):
            n = min(256, hidden - c)
            lhs = g[s]
            gate = dot_t(lhs, gw[c:c + n, :])
            up = dot_t(lhs, uw[c:c + n, :])
            h[:, c:c + n] = (gate / (1.0 + jnp.exp(-gate)) * up).astype(h.dtype)

        def columns(i, carry):
            at = pl.ds(pl.multiple_of(i * wide, 128), wide)
            p[s, :, at] = jnp.dot(
                h[...], dw[:, at], preferred_element_type=jnp.float32
            ).astype(p.dtype)
            return carry

        lax.fori_loop(0, width // wide, columns, 0)
        for k in range(1, xs):
            reduce_xa(k, s).start()

    for w in weights:
        w.wait()
    compute(z)

    def add_rows(count, target, parts):
        def body(i, carry):
            i = pl.multiple_of(i * 16, 16)
            total = None
            for part in parts:
                value = part(pl.ds(i, 16)).astype(jnp.float32)
                total = value if total is None else total + value
            target(i, total)
            return carry

        lax.fori_loop(0, count // 16, body, 0)

    def p_part(o, piece):
        base = p_base(piece)

        def read(at):
            return p[o, pl.ds(pl.multiple_of(base + at.start, 16), 16), :]

        def write(i, value):
            p[o, pl.ds(pl.multiple_of(base + i, 16), 16), :] = value.astype(p.dtype)

        return read, write

    def rz_part(d, o, piece):
        base = rz_base(piece)

        def read(at):
            return rz[d, o, pl.ds(pl.multiple_of(base + at.start, 16), 16), :]

        return read

    def from_x(ref, first):
        return lambda at: ref[pl.ds(pl.multiple_of(first + at.start, 16), 16), :]

    def rxa_parts(o, first):
        return [from_x(rxa.at[k - 1, o], first) for k in range(1, xs)]

    def rxb_parts(first):
        return [from_x(rxb.at[k - 1], first) for k in range(1, xs)]

    def step(t, carry):
        for d in (0, 1):
            s = z - t if d == 1 else z + t

            @pl.when((s >= 0) & (s < zs))
            def _():
                for unit in units:
                    gather_z(d, s, unit).wait_recv()

                    @pl.when(has_next(d))
                    def _():
                        gather_z(d, s, unit).start()
                    if unit is None:
                        for k in range(1, xs):
                            gather_xa(k, s, x).start()

        def slab(j, c):
            s = z + t * (1 - 2 * j)

            @pl.when((s >= 0) & (s < zs))
            def _():
                compute(s)
            return c

        lax.fori_loop(0, 2, slab, 0)

        for piece in [q for sx in range(xs) for q in b_pieces(sx)] + a_pieces():
            def flow(j, c):
                d = jnp.where(z < zs // 2, 1 - j, j)
                o = jnp.where(d == 0, zs - 1 - t, t)
                dist = jnp.where(d == 0, z - o, o - z)
                fed = jnp.where(d == 0, zs - 1 - z, z)

                @pl.when(dist > 0)
                def _():
                    parts = []
                    if piece[0] is None:
                        if piece[1] == 0:
                            for k in range(1, xs):
                                reduce_xa(k, o).wait_recv()
                        parts = rxa_parts(o, piece[1])

                    @pl.when(fed > 0)
                    def _():
                        reduce_z(d, o, piece).wait_recv()
                    read, write = p_part(o, piece)
                    add_rows(piece[2], write, [read, rz_part(d, o, piece)] + parts)
                    reduce_z(d, o, piece).start()
                return c

            lax.fori_loop(0, 2, flow, 0)
        return carry

    lax.fori_loop(1, zs, step, 0)

    def take(piece):
        for d in (0, 1):
            @pl.when(has_next(1 - d))
            def _():
                reduce_z(d, z, piece).wait_recv()

    for k in range(1, xs):
        for piece in b_pieces(other(k)):
            take(piece)
            read, write = p_part(z, piece)
            add_rows(piece[2], write, [read, rz_part(0, z, piece), rz_part(1, z, piece)])
        reduce_xb(k).start()

    def out_at(base):
        def write(i, value):
            out_ref[pl.ds(pl.multiple_of(base + i, 16), 16), :] = value.astype(out_ref.dtype)
        return write

    for k in range(1, xs):
        reduce_xa(k, z).wait_recv()
    for piece in a_pieces():
        take(piece)
        add_rows(
            piece[2], out_at(piece[1]),
            [p_part(z, piece)[0], rz_part(0, z, piece), rz_part(1, z, piece)]
            + rxa_parts(z, piece[1]),
        )
    for k in range(1, xs):
        reduce_xb(k).wait_recv()
    for piece in b_pieces(x):
        take(piece)
        add_rows(
            piece[2], out_at(ra + piece[1]),
            [p_part(z, piece)[0], rz_part(0, z, piece), rz_part(1, z, piece)]
            + rxb_parts(piece[1]),
        )

    for k in range(1, xs):
        gather_xb(k, x).wait_send()
        reduce_xb(k).wait_send()

    def sent(s, carry):
        for k in range(1, xs):
            gather_xa(k, s, x).wait_send()
            reduce_xa(k, s).wait_send()
        for d in (0, 1):
            behind = s <= z if d == 1 else s >= z
            ahead = s > z if d == 1 else s < z

            @pl.when(has_next(d) & behind)
            def _():
                for unit in units:
                    gather_z(d, s, unit).wait_send()

            @pl.when(ahead)
            def _():
                for piece in a_pieces() + [q for sx in range(xs) for q in b_pieces(sx)]:
                    reduce_z(d, s, piece).wait_send()
        return carry

    lax.fori_loop(0, zs, sent, 0)


def expert_sum(slot_rows, gate_weight, up_weight, down_weight, tensor):
    rows, width = slot_rows.shape
    hidden = gate_weight.shape[0]
    zs = ROWS_Z if tensor % ROWS_Z == 0 else 1
    xs = tensor // zs
    ra = rows * 5 // 8 // 16 * 16
    rb = rows - ra
    wide = 512 if width % 512 == 0 else 128
    dt = slot_rows.dtype
    dma = pltpu.SemaphoreType.DMA
    pieces = len(cuts(ra)) + xs * len(cuts(rb))
    flops = 6 * rows * tensor * width * hidden
    return pl.pallas_call(
        functools.partial(expert_kernel, zs, xs, ra, wide),
        out_shape=jax.ShapeDtypeStruct((rows, width), dt),
        in_specs=[pl.BlockSpec(memory_space=pltpu.VMEM)]
        + [pl.BlockSpec(memory_space=pl.ANY)] * 3,
        out_specs=pl.BlockSpec(memory_space=pltpu.VMEM),
        scratch_shapes=[
            pltpu.VMEM((zs, xs * rows, width), dt),
            pltpu.VMEM((zs, xs * rows, width), dt),
            pltpu.VMEM((2, zs, ra + xs * rb, width), dt),
            pltpu.VMEM((xs - 1, zs, ra, width), dt),
            pltpu.VMEM((xs - 1, rb, width), dt),
            pltpu.VMEM((xs * rows, hidden), dt),
            pltpu.VMEM(gate_weight.shape, dt),
            pltpu.VMEM(up_weight.shape, dt),
            pltpu.VMEM(down_weight.shape, dt),
            dma((3,)),
            dma((2, zs, xs + 1)), dma((zs, xs + 1)),
            dma((zs, xs - 1)), dma((zs, xs - 1)),
            dma((xs - 1,)), dma((xs - 1,)),
            dma((2, zs, pieces)), dma((2, zs, pieces)),
            dma((zs, xs - 1)), dma((zs, xs - 1)),
            dma((xs - 1,)), dma((xs - 1,)),
        ],
        compiler_params=pltpu.CompilerParams(
            collective_id=0, has_side_effects=True, vmem_limit_bytes=60 * 2**20
        ),
        cost_estimate=pl.CostEstimate(
            flops=flops, bytes_accessed=6 * width * hidden + 4 * rows * width,
            transcendentals=rows * tensor * hidden,
        ),
    )(slot_rows, gate_weight, up_weight, down_weight)


def on_device(tensor, tokens, expert_ids, gate_probs, gate_weight, up_weight, down_weight):
    count, width = tokens.shape
    spans = count // CT
    is_window = expert_ids == 0
    routed = jnp.any(is_window, axis=1)
    gate_share = jnp.sum(jnp.where(is_window, gate_probs, 0.0), axis=1)
    routed_blocks = routed.reshape(spans, CT)
    slot_place = jnp.cumsum(routed_blocks.astype(jnp.int32), axis=1) - 1
    selector = (
        (slot_place[:, None, :] == jnp.arange(CAP, dtype=jnp.int32)[None, :, None])
        & routed_blocks[:, None, :]
    ).astype(jnp.bfloat16)
    slot_rows = jnp.einsum(
        "bst,btd->bsd", selector, tokens.reshape(spans, CT, width),
        preferred_element_type=jnp.float32,
    ).astype(jnp.bfloat16)
    expert_out = expert_sum(
        slot_rows.reshape(spans * CAP, width), gate_weight.T, up_weight.T, down_weight, tensor
    )
    picked = jnp.einsum(
        "bst,bsd->btd", selector, expert_out.reshape(spans, CAP, width),
        preferred_element_type=jnp.float32,
    )
    mixed = gate_share.reshape(spans, CT)[:, :, None] * picked
    return mixed.astype(jnp.bfloat16).reshape(count, width)


def solution(mesh):
    in_specs = (
        P(("dp", "tensor"), None),
        P(("dp", "tensor"), None),
        P(("dp", "tensor"), None),
        P(None, "tensor"),
        P(None, "tensor"),
        P("tensor", None),
    )
    out_specs = P(("dp", "tensor"), None)
    return jax.shard_map(
        functools.partial(on_device, mesh.shape["tensor"]),
        mesh=mesh, in_specs=in_specs, out_specs=out_specs, check_vma=False,
    )
```

```python
import functools

import jax
import jax.numpy as jnp
from jax import lax
from jax.experimental import pallas as pl
from jax.experimental.pallas import tpu as pltpu
from jax.sharding import PartitionSpec as P

CT = 128
CAP = 32
ROWS_Z = 4
PIECE = 32
MESH = pl.DeviceIdType.MESH


def cuts(rows):
    return [(at, min(PIECE, rows - at)) for at in range(0, rows, PIECE)]


def dot_t(a, b):
    return lax.dot_general(
        a, b, (((1,), (1,)), ((), ())), preferred_element_type=jnp.float32
    )


def expert_kernel(
    zs, xs, ra, wide,
    slot_ref, gw_hbm, uw_hbm, dw_hbm, out_ref,
    g, p, rz, rxa, rxb, h, gw, uw, dw,
    wsem, agz_s, agz_r, axa_s, axa_r, axb_s, axb_r,
    rz_s, rz_r, rxa_s, rxa_r, rxb_s, rxb_r,
):
    rows, width = slot_ref.shape
    rb = rows - ra
    hidden = gw.shape[0]
    me = lax.axis_index("tensor")
    dp = lax.axis_index("dp")
    z = me // xs
    x = me % xs

    def dev(zz, xx):
        return (dp, zz * xs + xx)

    def a_rows(sx):
        return pl.ds(pl.multiple_of(sx * rows, 16), ra)

    def b_rows(sx):
        return pl.ds(pl.multiple_of(sx * rows + ra, 16), rb)

    def other(k):
        return (x + k) % xs

    def source(k):
        return (x + xs - k) % xs

    def unit_rows(unit):
        return a_rows(x) if unit is None else b_rows(unit)

    def unit_sem(unit):
        return 0 if unit is None else 1 + unit

    a_cuts = cuts(ra)
    b_cuts = cuts(rb)

    def a_pieces():
        return [(None, at, n, i) for i, (at, n) in enumerate(a_cuts)]

    def b_pieces(sx):
        return [
            (sx, at, n, len(a_cuts) + sx * len(b_cuts) + i)
            for i, (at, n) in enumerate(b_cuts)
        ]

    def p_base(piece):
        sx, at = piece[:2]
        return x * rows + at if sx is None else sx * rows + ra + at

    def rz_base(piece):
        sx, at = piece[:2]
        return at if sx is None else ra + sx * rb + at

    units = [None] + list(range(xs))

    def copy(src, dst, s, r, to):
        return pltpu.make_async_remote_copy(
            src_ref=src, dst_ref=dst, send_sem=s, recv_sem=r,
            device_id=to, device_id_type=MESH,
        )

    def gather_z(d, s, unit):
        part = g.at[s, unit_rows(unit)]
        i = unit_sem(unit)
        return copy(part, part, agz_s.at[d, s, i], agz_r.at[s, i], dev(z + 2 * d - 1, x))

    def gather_xa(k, s, sx):
        part = g.at[s, a_rows(sx)]
        return copy(part, part, axa_s.at[s, k - 1], axa_r.at[s, k - 1], dev(z, other(k)))

    def gather_xb(k, sx):
        part = g.at[z, b_rows(sx)]
        return copy(part, part, axb_s.at[k - 1], axb_r.at[k - 1], dev(z, other(k)))

    def reduce_xa(k, s):
        return copy(
            p.at[s, a_rows(other(k))], rxa.at[k - 1, s],
            rxa_s.at[s, k - 1], rxa_r.at[s, k - 1], dev(z, other(k)),
        )

    def reduce_xb(k):
        return copy(
            p.at[z, b_rows(other(k))], rxb.at[k - 1],
            rxb_s.at[k - 1], rxb_r.at[k - 1], dev(z, other(k)),
        )

    def reduce_z(d, o, piece):
        n, i = piece[2:]
        return copy(
            p.at[o, pl.ds(pl.multiple_of(p_base(piece), 16), n)],
            rz.at[d, o, pl.ds(pl.multiple_of(rz_base(piece), 16), n)],
            rz_s.at[d, o, i], rz_r.at[d, o, i], dev(z + 2 * d - 1, x),
        )

    def has_next(d):
        return z < zs - 1 if d == 1 else z > 0

    weights = [
        pltpu.make_async_copy(a, b, wsem.at[i])
        for i, (a, b) in enumerate(((gw_hbm, gw), (uw_hbm, uw), (dw_hbm, dw)))
    ]
    for w in weights:
        w.start()

    barrier = pltpu.get_barrier_semaphore()
    for d in (0, 1):
        @pl.when(has_next(d))
        def _():
            pl.semaphore_signal(barrier, inc=1, device_id=dev(z + 2 * d - 1, x), device_id_type=MESH)
    for k in range(1, xs):
        pl.semaphore_signal(barrier, inc=1, device_id=dev(z, other(k)), device_id_type=MESH)
    g[z, pl.ds(pl.multiple_of(x * rows, 16), rows), :] = slot_ref[...]
    ends = (z == 0).astype(jnp.int32) + (z == zs - 1).astype(jnp.int32)
    pl.semaphore_wait(barrier, xs + 1 - ends)

    for k in range(1, xs):
        gather_xb(k, x).start()
    for d in (0, 1):
        @pl.when(has_next(d))
        def _():
            gather_z(d, z, None).start()
            gather_z(d, z, x).start()
    for k in range(1, xs):
        gather_xa(k, z, x).start()

    @pl.when(z == zs - 1)
    def _():
        rz[0] = jnp.zeros(rz.shape[1:], rz.dtype)

    @pl.when(z == 0)
    def _():
        rz[1] = jnp.zeros(rz.shape[1:], rz.dtype)

    for k in range(1, xs):
        gather_xb(k, source(k)).wait_recv()
        for d in (0, 1):
            @pl.when(has_next(d))
            def _():
                gather_z(d, z, source(k)).start()

    def compute(s):
        for k in range(1, xs):
            gather_xa(k, s, source(k)).wait_recv()
        for c in range(0, hidden, 256):
            n = min(256, hidden - c)
            lhs = g[s]
            gate = dot_t(lhs, gw[c:c + n, :])
            up = dot_t(lhs, uw[c:c + n, :])
            h[:, c:c + n] = (gate / (1.0 + jnp.exp(-gate)) * up).astype(h.dtype)

        def columns(i, carry):
            at = pl.ds(pl.multiple_of(i * wide, 128), wide)
            p[s, :, at] = jnp.dot(
                h[...], dw[:, at], preferred_element_type=jnp.float32
            ).astype(p.dtype)
            return carry

        lax.fori_loop(0, width // wide, columns, 0)
        for k in range(1, xs):
            reduce_xa(k, s).start()

    for w in weights:
        w.wait()
    compute(z)

    def add_rows(count, target, parts):
        def body(i, carry):
            i = pl.multiple_of(i * 16, 16)
            total = None
            for part in parts:
                value = part(pl.ds(i, 16)).astype(jnp.float32)
                total = value if total is None else total + value
            target(i, total)
            return carry

        lax.fori_loop(0, count // 16, body, 0)

    def p_part(o, piece):
        base = p_base(piece)

        def read(at):
            return p[o, pl.ds(pl.multiple_of(base + at.start, 16), 16), :]

        def write(i, value):
            p[o, pl.ds(pl.multiple_of(base + i, 16), 16), :] = value.astype(p.dtype)

        return read, write

    def rz_part(d, o, piece):
        base = rz_base(piece)

        def read(at):
            return rz[d, o, pl.ds(pl.multiple_of(base + at.start, 16), 16), :]

        return read

    def from_x(ref, first):
        return lambda at: ref[pl.ds(pl.multiple_of(first + at.start, 16), 16), :]

    def rxa_parts(o, first):
        return [from_x(rxa.at[k - 1, o], first) for k in range(1, xs)]

    def rxb_parts(first):
        return [from_x(rxb.at[k - 1], first) for k in range(1, xs)]

    def step(t, carry):
        for unit in units:
            for d in (0, 1):
                s = z - t if d == 1 else z + t

                @pl.when((s >= 0) & (s < zs))
                def _():
                    gather_z(d, s, unit).wait_recv()

                    @pl.when(has_next(d))
                    def _():
                        gather_z(d, s, unit).start()
                    if unit is None:
                        for k in range(1, xs):
                            gather_xa(k, s, x).start()

        def slab(j, c):
            far = jnp.where(z < zs // 2, 1, -1)
            s = jnp.where(j == 0, z - far * (t - 1), z + far * t)

            @pl.when((s >= 0) & (s < zs) & (j + t >= 2))
            def _():
                compute(s)
            return c

        lax.fori_loop(0, 2, slab, 0)

        for piece in [q for sx in range(xs) for q in b_pieces(sx)] + a_pieces():
            def flow(j, c):
                d = jnp.where(z < zs // 2, 1 - j, j)
                o = jnp.where(d == 0, zs - 1 - t, t)
                dist = jnp.where(d == 0, z - o, o - z)
                fed = jnp.where(d == 0, zs - 1 - z, z)

                @pl.when(dist > 0)
                def _():
                    parts = []
                    if piece[0] is None:
                        if piece[1] == 0:
                            for k in range(1, xs):
                                reduce_xa(k, o).wait_recv()
                        parts = rxa_parts(o, piece[1])

                    @pl.when(fed > 0)
                    def _():
                        reduce_z(d, o, piece).wait_recv()
                    read, write = p_part(o, piece)
                    add_rows(piece[2], write, [read, rz_part(d, o, piece)] + parts)
                    reduce_z(d, o, piece).start()
                return c

            lax.fori_loop(0, 2, flow, 0)
        return carry

    lax.fori_loop(1, zs, step, 0)

    def take(piece):
        for d in (0, 1):
            @pl.when(has_next(1 - d))
            def _():
                reduce_z(d, z, piece).wait_recv()

    for k in range(1, xs):
        for piece in b_pieces(other(k)):
            take(piece)
            read, write = p_part(z, piece)
            add_rows(piece[2], write, [read, rz_part(0, z, piece), rz_part(1, z, piece)])
        reduce_xb(k).start()

    def out_at(base):
        def write(i, value):
            out_ref[pl.ds(pl.multiple_of(base + i, 16), 16), :] = value.astype(out_ref.dtype)
        return write

    for k in range(1, xs):
        reduce_xa(k, z).wait_recv()
    for piece in a_pieces():
        take(piece)
        add_rows(
            piece[2], out_at(piece[1]),
            [p_part(z, piece)[0], rz_part(0, z, piece), rz_part(1, z, piece)]
            + rxa_parts(z, piece[1]),
        )
    for k in range(1, xs):
        reduce_xb(k).wait_recv()
    for piece in b_pieces(x):
        take(piece)
        add_rows(
            piece[2], out_at(ra + piece[1]),
            [p_part(z, piece)[0], rz_part(0, z, piece), rz_part(1, z, piece)]
            + rxb_parts(piece[1]),
        )

    for k in range(1, xs):
        gather_xb(k, x).wait_send()
        reduce_xb(k).wait_send()

    def sent(s, carry):
        for k in range(1, xs):
            gather_xa(k, s, x).wait_send()
            reduce_xa(k, s).wait_send()
        for d in (0, 1):
            behind = s <= z if d == 1 else s >= z
            ahead = s > z if d == 1 else s < z

            @pl.when(has_next(d) & behind)
            def _():
                for unit in units:
                    gather_z(d, s, unit).wait_send()

            @pl.when(ahead)
            def _():
                for piece in a_pieces() + [q for sx in range(xs) for q in b_pieces(sx)]:
                    reduce_z(d, s, piece).wait_send()
        return carry

    lax.fori_loop(0, zs, sent, 0)


def expert_sum(slot_rows, gate_weight, up_weight, down_weight, tensor):
    rows, width = slot_rows.shape
    hidden = gate_weight.shape[0]
    zs = ROWS_Z if tensor % ROWS_Z == 0 else 1
    xs = tensor // zs
    ra = rows * 5 // 8 // 16 * 16
    rb = rows - ra
    wide = 512 if width % 512 == 0 else 128
    dt = slot_rows.dtype
    dma = pltpu.SemaphoreType.DMA
    pieces = len(cuts(ra)) + xs * len(cuts(rb))
    flops = 6 * rows * tensor * width * hidden
    return pl.pallas_call(
        functools.partial(expert_kernel, zs, xs, ra, wide),
        out_shape=jax.ShapeDtypeStruct((rows, width), dt),
        in_specs=[pl.BlockSpec(memory_space=pltpu.VMEM)]
        + [pl.BlockSpec(memory_space=pl.ANY)] * 3,
        out_specs=pl.BlockSpec(memory_space=pltpu.VMEM),
        scratch_shapes=[
            pltpu.VMEM((zs, xs * rows, width), dt),
            pltpu.VMEM((zs, xs * rows, width), dt),
            pltpu.VMEM((2, zs, ra + xs * rb, width), dt),
            pltpu.VMEM((xs - 1, zs, ra, width), dt),
            pltpu.VMEM((xs - 1, rb, width), dt),
            pltpu.VMEM((xs * rows, hidden), dt),
            pltpu.VMEM(gate_weight.shape, dt),
            pltpu.VMEM(up_weight.shape, dt),
            pltpu.VMEM(down_weight.shape, dt),
            dma((3,)),
            dma((2, zs, xs + 1)), dma((zs, xs + 1)),
            dma((zs, xs - 1)), dma((zs, xs - 1)),
            dma((xs - 1,)), dma((xs - 1,)),
            dma((2, zs, pieces)), dma((2, zs, pieces)),
            dma((zs, xs - 1)), dma((zs, xs - 1)),
            dma((xs - 1,)), dma((xs - 1,)),
        ],
        compiler_params=pltpu.CompilerParams(
            collective_id=0, has_side_effects=True, vmem_limit_bytes=60 * 2**20
        ),
        cost_estimate=pl.CostEstimate(
            flops=flops, bytes_accessed=6 * width * hidden + 4 * rows * width,
            transcendentals=rows * tensor * hidden,
        ),
    )(slot_rows, gate_weight, up_weight, down_weight)


def on_device(tensor, tokens, expert_ids, gate_probs, gate_weight, up_weight, down_weight):
    count, width = tokens.shape
    spans = count // CT
    is_window = expert_ids == 0
    routed = jnp.any(is_window, axis=1)
    gate_share = jnp.sum(jnp.where(is_window, gate_probs, 0.0), axis=1)
    routed_blocks = routed.reshape(spans, CT)
    slot_place = jnp.cumsum(routed_blocks.astype(jnp.int32), axis=1) - 1
    selector = (
        (slot_place[:, None, :] == jnp.arange(CAP, dtype=jnp.int32)[None, :, None])
        & routed_blocks[:, None, :]
    ).astype(jnp.bfloat16)
    slot_rows = jnp.einsum(
        "bst,btd->bsd", selector, tokens.reshape(spans, CT, width),
        preferred_element_type=jnp.float32,
    ).astype(jnp.bfloat16)
    expert_out = expert_sum(
        slot_rows.reshape(spans * CAP, width), gate_weight.T, up_weight.T, down_weight, tensor
    )
    picked = jnp.einsum(
        "bst,bsd->btd", selector, expert_out.reshape(spans, CAP, width),
        preferred_element_type=jnp.float32,
    )
    mixed = gate_share.reshape(spans, CT)[:, :, None] * picked
    return mixed.astype(jnp.bfloat16).reshape(count, width)


def solution(mesh):
    in_specs = (
        P(("dp", "tensor"), None),
        P(("dp", "tensor"), None),
        P(("dp", "tensor"), None),
        P(None, "tensor"),
        P(None, "tensor"),
        P("tensor", None),
    )
    out_specs = P(("dp", "tensor"), None)
    return jax.shard_map(
        functools.partial(on_device, mesh.shape["tensor"]),
        mesh=mesh, in_specs=in_specs, out_specs=out_specs, check_vma=False,
    )
```

```python
import functools

import jax
import jax.numpy as jnp
from jax import lax
from jax.experimental import pallas as pl
from jax.experimental.pallas import tpu as pltpu
from jax.sharding import PartitionSpec as P

CT = 128
CAP = 32
ROWS_Z = 4
PIECE = 16
MESH = pl.DeviceIdType.MESH


def cuts(rows):
    return [(at, min(PIECE, rows - at)) for at in range(0, rows, PIECE)]


def dot_t(a, b):
    return lax.dot_general(
        a, b, (((1,), (1,)), ((), ())), preferred_element_type=jnp.float32
    )


def expert_kernel(
    zs, xs, ra, wide,
    slot_ref, gw_hbm, uw_hbm, dw_hbm, out_ref,
    g, p, rz, rxa, rxb, h, gw, uw, dw,
    wsem, agz_s, agz_r, axa_s, axa_r, axb_s, axb_r,
    rz_s, rz_r, rxa_s, rxa_r, rxb_s, rxb_r,
):
    rows, width = slot_ref.shape
    rb = rows - ra
    hidden = gw.shape[0]
    me = lax.axis_index("tensor")
    dp = lax.axis_index("dp")
    z = me // xs
    x = me % xs

    def dev(zz, xx):
        return (dp, zz * xs + xx)

    def a_rows(sx):
        return pl.ds(pl.multiple_of(sx * rows, 16), ra)

    def b_rows(sx):
        return pl.ds(pl.multiple_of(sx * rows + ra, 16), rb)

    def other(k):
        return (x + k) % xs

    def source(k):
        return (x + xs - k) % xs

    def unit_rows(unit):
        return a_rows(x) if unit is None else b_rows(unit)

    def unit_sem(unit):
        return 0 if unit is None else 1 + unit

    a_cuts = cuts(ra)
    b_cuts = cuts(rb)

    def a_pieces():
        return [(None, at, n, i) for i, (at, n) in enumerate(a_cuts)]

    def b_pieces(sx):
        return [
            (sx, at, n, len(a_cuts) + sx * len(b_cuts) + i)
            for i, (at, n) in enumerate(b_cuts)
        ]

    def p_base(piece):
        sx, at = piece[:2]
        return x * rows + at if sx is None else sx * rows + ra + at

    def rz_base(piece):
        sx, at = piece[:2]
        return at if sx is None else ra + sx * rb + at

    units = [None] + list(range(xs))

    def copy(src, dst, s, r, to):
        return pltpu.make_async_remote_copy(
            src_ref=src, dst_ref=dst, send_sem=s, recv_sem=r,
            device_id=to, device_id_type=MESH,
        )

    def gather_z(d, s, unit):
        part = g.at[s, unit_rows(unit)]
        i = unit_sem(unit)
        return copy(part, part, agz_s.at[d, s, i], agz_r.at[s, i], dev(z + 2 * d - 1, x))

    def gather_xa(k, s, sx):
        part = g.at[s, a_rows(sx)]
        return copy(part, part, axa_s.at[s, k - 1], axa_r.at[s, k - 1], dev(z, other(k)))

    def gather_xb(k, sx):
        part = g.at[z, b_rows(sx)]
        return copy(part, part, axb_s.at[k - 1], axb_r.at[k - 1], dev(z, other(k)))

    def reduce_xa(k, s):
        return copy(
            p.at[s, a_rows(other(k))], rxa.at[k - 1, s],
            rxa_s.at[s, k - 1], rxa_r.at[s, k - 1], dev(z, other(k)),
        )

    def reduce_xb(k):
        return copy(
            p.at[z, b_rows(other(k))], rxb.at[k - 1],
            rxb_s.at[k - 1], rxb_r.at[k - 1], dev(z, other(k)),
        )

    def reduce_z(d, o, piece):
        n, i = piece[2:]
        return copy(
            p.at[o, pl.ds(pl.multiple_of(p_base(piece), 16), n)],
            rz.at[d, o, pl.ds(pl.multiple_of(rz_base(piece), 16), n)],
            rz_s.at[d, o, i], rz_r.at[d, o, i], dev(z + 2 * d - 1, x),
        )

    def has_next(d):
        return z < zs - 1 if d == 1 else z > 0

    weights = [
        pltpu.make_async_copy(a, b, wsem.at[i])
        for i, (a, b) in enumerate(((gw_hbm, gw), (uw_hbm, uw), (dw_hbm, dw)))
    ]
    for w in weights:
        w.start()

    barrier = pltpu.get_barrier_semaphore()
    for d in (0, 1):
        @pl.when(has_next(d))
        def _():
            pl.semaphore_signal(barrier, inc=1, device_id=dev(z + 2 * d - 1, x), device_id_type=MESH)
    for k in range(1, xs):
        pl.semaphore_signal(barrier, inc=1, device_id=dev(z, other(k)), device_id_type=MESH)
    g[z, pl.ds(pl.multiple_of(x * rows, 16), rows), :] = slot_ref[...]
    ends = (z == 0).astype(jnp.int32) + (z == zs - 1).astype(jnp.int32)
    pl.semaphore_wait(barrier, xs + 1 - ends)

    for k in range(1, xs):
        gather_xb(k, x).start()
    for d in (0, 1):
        @pl.when(has_next(d))
        def _():
            gather_z(d, z, None).start()
            gather_z(d, z, x).start()
    for k in range(1, xs):
        gather_xa(k, z, x).start()

    @pl.when(z == zs - 1)
    def _():
        rz[0] = jnp.zeros(rz.shape[1:], rz.dtype)

    @pl.when(z == 0)
    def _():
        rz[1] = jnp.zeros(rz.shape[1:], rz.dtype)

    for k in range(1, xs):
        gather_xb(k, source(k)).wait_recv()
        for d in (0, 1):
            @pl.when(has_next(d))
            def _():
                gather_z(d, z, source(k)).start()

    def compute(s):
        for k in range(1, xs):
            gather_xa(k, s, source(k)).wait_recv()
        for c in range(0, hidden, 256):
            n = min(256, hidden - c)
            lhs = g[s]
            gate = dot_t(lhs, gw[c:c + n, :])
            up = dot_t(lhs, uw[c:c + n, :])
            h[:, c:c + n] = (gate / (1.0 + jnp.exp(-gate)) * up).astype(h.dtype)

        def columns(i, carry):
            at = pl.ds(pl.multiple_of(i * wide, 128), wide)
            p[s, :, at] = jnp.dot(
                h[...], dw[:, at], preferred_element_type=jnp.float32
            ).astype(p.dtype)
            return carry

        lax.fori_loop(0, width // wide, columns, 0)
        for k in range(1, xs):
            reduce_xa(k, s).start()

    for w in weights:
        w.wait()
    compute(z)

    def add_rows(count, target, parts):
        def body(i, carry):
            i = pl.multiple_of(i * 16, 16)
            total = None
            for part in parts:
                value = part(pl.ds(i, 16)).astype(jnp.float32)
                total = value if total is None else total + value
            target(i, total)
            return carry

        lax.fori_loop(0, count // 16, body, 0)

    def p_part(o, piece):
        base = p_base(piece)

        def read(at):
            return p[o, pl.ds(pl.multiple_of(base + at.start, 16), 16), :]

        def write(i, value):
            p[o, pl.ds(pl.multiple_of(base + i, 16), 16), :] = value.astype(p.dtype)

        return read, write

    def rz_part(d, o, piece):
        base = rz_base(piece)

        def read(at):
            return rz[d, o, pl.ds(pl.multiple_of(base + at.start, 16), 16), :]

        return read

    def from_x(ref, first):
        return lambda at: ref[pl.ds(pl.multiple_of(first + at.start, 16), 16), :]

    def rxa_parts(o, first):
        return [from_x(rxa.at[k - 1, o], first) for k in range(1, xs)]

    def rxb_parts(first):
        return [from_x(rxb.at[k - 1], first) for k in range(1, xs)]

    def step(t, carry):
        for unit in units:
            for d in (0, 1):
                s = z - t if d == 1 else z + t

                @pl.when((s >= 0) & (s < zs))
                def _():
                    gather_z(d, s, unit).wait_recv()

                    @pl.when(has_next(d))
                    def _():
                        gather_z(d, s, unit).start()
                    if unit is None:
                        for k in range(1, xs):
                            gather_xa(k, s, x).start()

        def slab(j, c):
            far = jnp.where(z < zs // 2, 1, -1)
            s = jnp.where(j == 0, z - far * (t - 1), z + far * t)

            @pl.when((s >= 0) & (s < zs) & (j + t >= 2))
            def _():
                compute(s)
            return c

        lax.fori_loop(0, 2, slab, 0)

        for piece in [q for sx in range(xs) for q in b_pieces(sx)] + a_pieces():
            def flow(j, c):
                d = jnp.where(z < zs // 2, 1 - j, j)
                o = jnp.where(d == 0, zs - 1 - t, t)
                dist = jnp.where(d == 0, z - o, o - z)
                fed = jnp.where(d == 0, zs - 1 - z, z)

                @pl.when(dist > 0)
                def _():
                    parts = []
                    if piece[0] is None:
                        if piece[1] == 0:
                            for k in range(1, xs):
                                reduce_xa(k, o).wait_recv()
                        parts = rxa_parts(o, piece[1])

                    @pl.when(fed > 0)
                    def _():
                        reduce_z(d, o, piece).wait_recv()
                    read, write = p_part(o, piece)
                    add_rows(piece[2], write, [read, rz_part(d, o, piece)] + parts)
                    reduce_z(d, o, piece).start()
                return c

            lax.fori_loop(0, 2, flow, 0)
        return carry

    lax.fori_loop(1, zs, step, 0)

    def take(piece):
        for d in (0, 1):
            @pl.when(has_next(1 - d))
            def _():
                reduce_z(d, z, piece).wait_recv()

    for k in range(1, xs):
        for piece in b_pieces(other(k)):
            take(piece)
            read, write = p_part(z, piece)
            add_rows(piece[2], write, [read, rz_part(0, z, piece), rz_part(1, z, piece)])
        reduce_xb(k).start()

    def out_at(base):
        def write(i, value):
            out_ref[pl.ds(pl.multiple_of(base + i, 16), 16), :] = value.astype(out_ref.dtype)
        return write

    for k in range(1, xs):
        reduce_xa(k, z).wait_recv()
    for piece in a_pieces():
        take(piece)
        add_rows(
            piece[2], out_at(piece[1]),
            [p_part(z, piece)[0], rz_part(0, z, piece), rz_part(1, z, piece)]
            + rxa_parts(z, piece[1]),
        )
    for k in range(1, xs):
        reduce_xb(k).wait_recv()
    for piece in b_pieces(x):
        take(piece)
        add_rows(
            piece[2], out_at(ra + piece[1]),
            [p_part(z, piece)[0], rz_part(0, z, piece), rz_part(1, z, piece)]
            + rxb_parts(piece[1]),
        )

    for k in range(1, xs):
        gather_xb(k, x).wait_send()
        reduce_xb(k).wait_send()

    def sent(s, carry):
        for k in range(1, xs):
            gather_xa(k, s, x).wait_send()
            reduce_xa(k, s).wait_send()
        for d in (0, 1):
            behind = s <= z if d == 1 else s >= z
            ahead = s > z if d == 1 else s < z

            @pl.when(has_next(d) & behind)
            def _():
                for unit in units:
                    gather_z(d, s, unit).wait_send()

            @pl.when(ahead)
            def _():
                for piece in a_pieces() + [q for sx in range(xs) for q in b_pieces(sx)]:
                    reduce_z(d, s, piece).wait_send()
        return carry

    lax.fori_loop(0, zs, sent, 0)


def expert_sum(slot_rows, gate_weight, up_weight, down_weight, tensor):
    rows, width = slot_rows.shape
    hidden = gate_weight.shape[0]
    zs = ROWS_Z if tensor % ROWS_Z == 0 else 1
    xs = tensor // zs
    ra = rows * 5 // 8 // 16 * 16
    rb = rows - ra
    wide = 512 if width % 512 == 0 else 128
    dt = slot_rows.dtype
    dma = pltpu.SemaphoreType.DMA
    pieces = len(cuts(ra)) + xs * len(cuts(rb))
    flops = 6 * rows * tensor * width * hidden
    return pl.pallas_call(
        functools.partial(expert_kernel, zs, xs, ra, wide),
        out_shape=jax.ShapeDtypeStruct((rows, width), dt),
        in_specs=[pl.BlockSpec(memory_space=pltpu.VMEM)]
        + [pl.BlockSpec(memory_space=pl.ANY)] * 3,
        out_specs=pl.BlockSpec(memory_space=pltpu.VMEM),
        scratch_shapes=[
            pltpu.VMEM((zs, xs * rows, width), dt),
            pltpu.VMEM((zs, xs * rows, width), dt),
            pltpu.VMEM((2, zs, ra + xs * rb, width), dt),
            pltpu.VMEM((xs - 1, zs, ra, width), dt),
            pltpu.VMEM((xs - 1, rb, width), dt),
            pltpu.VMEM((xs * rows, hidden), dt),
            pltpu.VMEM(gate_weight.shape, dt),
            pltpu.VMEM(up_weight.shape, dt),
            pltpu.VMEM(down_weight.shape, dt),
            dma((3,)),
            dma((2, zs, xs + 1)), dma((zs, xs + 1)),
            dma((zs, xs - 1)), dma((zs, xs - 1)),
            dma((xs - 1,)), dma((xs - 1,)),
            dma((2, zs, pieces)), dma((2, zs, pieces)),
            dma((zs, xs - 1)), dma((zs, xs - 1)),
            dma((xs - 1,)), dma((xs - 1,)),
        ],
        compiler_params=pltpu.CompilerParams(
            collective_id=0, has_side_effects=True, vmem_limit_bytes=60 * 2**20
        ),
        cost_estimate=pl.CostEstimate(
            flops=flops, bytes_accessed=6 * width * hidden + 4 * rows * width,
            transcendentals=rows * tensor * hidden,
        ),
    )(slot_rows, gate_weight, up_weight, down_weight)


def on_device(tensor, tokens, expert_ids, gate_probs, gate_weight, up_weight, down_weight):
    count, width = tokens.shape
    spans = count // CT
    is_window = expert_ids == 0
    routed = jnp.any(is_window, axis=1)
    gate_share = jnp.sum(jnp.where(is_window, gate_probs, 0.0), axis=1)
    routed_blocks = routed.reshape(spans, CT)
    slot_place = jnp.cumsum(routed_blocks.astype(jnp.int32), axis=1) - 1
    selector = (
        (slot_place[:, None, :] == jnp.arange(CAP, dtype=jnp.int32)[None, :, None])
        & routed_blocks[:, None, :]
    ).astype(jnp.bfloat16)
    slot_rows = jnp.einsum(
        "bst,btd->bsd", selector, tokens.reshape(spans, CT, width),
        preferred_element_type=jnp.float32,
    ).astype(jnp.bfloat16)
    expert_out = expert_sum(
        slot_rows.reshape(spans * CAP, width), gate_weight.T, up_weight.T, down_weight, tensor
    )
    picked = jnp.einsum(
        "bst,bsd->btd", selector, expert_out.reshape(spans, CAP, width),
        preferred_element_type=jnp.float32,
    )
    mixed = gate_share.reshape(spans, CT)[:, :, None] * picked
    return mixed.astype(jnp.bfloat16).reshape(count, width)


def solution(mesh):
    in_specs = (
        P(("dp", "tensor"), None),
        P(("dp", "tensor"), None),
        P(("dp", "tensor"), None),
        P(None, "tensor"),
        P(None, "tensor"),
        P("tensor", None),
    )
    out_specs = P(("dp", "tensor"), None)
    return jax.shard_map(
        functools.partial(on_device, mesh.shape["tensor"]),
        mesh=mesh, in_specs=in_specs, out_specs=out_specs, check_vma=False,
    )
```

```python
import functools

import jax
import jax.numpy as jnp
from jax import lax
from jax.experimental import pallas as pl
from jax.experimental.pallas import tpu as pltpu
from jax.sharding import PartitionSpec as P

CT = 128
CAP = 32
ROWS_Z = 4
PIECE = 48
MESH = pl.DeviceIdType.MESH


def cuts(rows):
    return [(at, min(PIECE, rows - at)) for at in range(0, rows, PIECE)]


def dot_t(a, b):
    return lax.dot_general(
        a, b, (((1,), (1,)), ((), ())), preferred_element_type=jnp.float32
    )


def expert_kernel(
    zs, xs, ra, wide,
    slot_ref, gw_hbm, uw_hbm, dw_hbm, out_ref,
    g, p, rz, rxa, rxb, h, gw, uw, dw,
    wsem, agz_s, agz_r, axa_s, axa_r, axb_s, axb_r,
    rz_s, rz_r, rxa_s, rxa_r, rxb_s, rxb_r,
):
    rows, width = slot_ref.shape
    rb = rows - ra
    hidden = gw.shape[0]
    me = lax.axis_index("tensor")
    dp = lax.axis_index("dp")
    z = me // xs
    x = me % xs

    def dev(zz, xx):
        return (dp, zz * xs + xx)

    def a_rows(sx):
        return pl.ds(pl.multiple_of(sx * rows, 16), ra)

    def b_rows(sx):
        return pl.ds(pl.multiple_of(sx * rows + ra, 16), rb)

    def other(k):
        return (x + k) % xs

    def source(k):
        return (x + xs - k) % xs

    def unit_rows(unit):
        return a_rows(x) if unit is None else b_rows(unit)

    def unit_sem(unit):
        return 0 if unit is None else 1 + unit

    a_cuts = cuts(ra)
    b_cuts = cuts(rb)

    def a_pieces():
        return [(None, at, n, i) for i, (at, n) in enumerate(a_cuts)]

    def b_pieces(sx):
        return [
            (sx, at, n, len(a_cuts) + sx * len(b_cuts) + i)
            for i, (at, n) in enumerate(b_cuts)
        ]

    def p_base(piece):
        sx, at = piece[:2]
        return x * rows + at if sx is None else sx * rows + ra + at

    def rz_base(piece):
        sx, at = piece[:2]
        return at if sx is None else ra + sx * rb + at

    units = [None] + list(range(xs))

    def copy(src, dst, s, r, to):
        return pltpu.make_async_remote_copy(
            src_ref=src, dst_ref=dst, send_sem=s, recv_sem=r,
            device_id=to, device_id_type=MESH,
        )

    def gather_z(d, s, unit):
        part = g.at[s, unit_rows(unit)]
        i = unit_sem(unit)
        return copy(part, part, agz_s.at[d, s, i], agz_r.at[s, i], dev(z + 2 * d - 1, x))

    def gather_xa(k, s, sx):
        part = g.at[s, a_rows(sx)]
        return copy(part, part, axa_s.at[s, k - 1], axa_r.at[s, k - 1], dev(z, other(k)))

    def gather_xb(k, sx):
        part = g.at[z, b_rows(sx)]
        return copy(part, part, axb_s.at[k - 1], axb_r.at[k - 1], dev(z, other(k)))

    def reduce_xa(k, s):
        return copy(
            p.at[s, a_rows(other(k))], rxa.at[k - 1, s],
            rxa_s.at[s, k - 1], rxa_r.at[s, k - 1], dev(z, other(k)),
        )

    def reduce_xb(k):
        return copy(
            p.at[z, b_rows(other(k))], rxb.at[k - 1],
            rxb_s.at[k - 1], rxb_r.at[k - 1], dev(z, other(k)),
        )

    def reduce_z(d, o, piece):
        n, i = piece[2:]
        return copy(
            p.at[o, pl.ds(pl.multiple_of(p_base(piece), 16), n)],
            rz.at[d, o, pl.ds(pl.multiple_of(rz_base(piece), 16), n)],
            rz_s.at[d, o, i], rz_r.at[d, o, i], dev(z + 2 * d - 1, x),
        )

    def has_next(d):
        return z < zs - 1 if d == 1 else z > 0

    weights = [
        pltpu.make_async_copy(a, b, wsem.at[i])
        for i, (a, b) in enumerate(((gw_hbm, gw), (uw_hbm, uw), (dw_hbm, dw)))
    ]
    for w in weights:
        w.start()

    barrier = pltpu.get_barrier_semaphore()
    for d in (0, 1):
        @pl.when(has_next(d))
        def _():
            pl.semaphore_signal(barrier, inc=1, device_id=dev(z + 2 * d - 1, x), device_id_type=MESH)
    for k in range(1, xs):
        pl.semaphore_signal(barrier, inc=1, device_id=dev(z, other(k)), device_id_type=MESH)
    g[z, pl.ds(pl.multiple_of(x * rows, 16), rows), :] = slot_ref[...]
    ends = (z == 0).astype(jnp.int32) + (z == zs - 1).astype(jnp.int32)
    pl.semaphore_wait(barrier, xs + 1 - ends)

    for k in range(1, xs):
        gather_xb(k, x).start()
    for d in (0, 1):
        @pl.when(has_next(d))
        def _():
            gather_z(d, z, None).start()
            gather_z(d, z, x).start()
    for k in range(1, xs):
        gather_xa(k, z, x).start()

    @pl.when(z == zs - 1)
    def _():
        rz[0] = jnp.zeros(rz.shape[1:], rz.dtype)

    @pl.when(z == 0)
    def _():
        rz[1] = jnp.zeros(rz.shape[1:], rz.dtype)

    for k in range(1, xs):
        gather_xb(k, source(k)).wait_recv()
        for d in (0, 1):
            @pl.when(has_next(d))
            def _():
                gather_z(d, z, source(k)).start()

    def compute(s):
        for k in range(1, xs):
            gather_xa(k, s, source(k)).wait_recv()
        for c in range(0, hidden, 256):
            n = min(256, hidden - c)
            lhs = g[s]
            gate = dot_t(lhs, gw[c:c + n, :])
            up = dot_t(lhs, uw[c:c + n, :])
            h[:, c:c + n] = (gate / (1.0 + jnp.exp(-gate)) * up).astype(h.dtype)

        def columns(i, carry):
            at = pl.ds(pl.multiple_of(i * wide, 128), wide)
            p[s, :, at] = jnp.dot(
                h[...], dw[:, at], preferred_element_type=jnp.float32
            ).astype(p.dtype)
            return carry

        lax.fori_loop(0, width // wide, columns, 0)
        for k in range(1, xs):
            reduce_xa(k, s).start()

    for w in weights:
        w.wait()
    compute(z)

    def add_rows(count, target, parts):
        def body(i, carry):
            i = pl.multiple_of(i * 16, 16)
            total = None
            for part in parts:
                value = part(pl.ds(i, 16)).astype(jnp.float32)
                total = value if total is None else total + value
            target(i, total)
            return carry

        lax.fori_loop(0, count // 16, body, 0)

    def p_part(o, piece):
        base = p_base(piece)

        def read(at):
            return p[o, pl.ds(pl.multiple_of(base + at.start, 16), 16), :]

        def write(i, value):
            p[o, pl.ds(pl.multiple_of(base + i, 16), 16), :] = value.astype(p.dtype)

        return read, write

    def rz_part(d, o, piece):
        base = rz_base(piece)

        def read(at):
            return rz[d, o, pl.ds(pl.multiple_of(base + at.start, 16), 16), :]

        return read

    def from_x(ref, first):
        return lambda at: ref[pl.ds(pl.multiple_of(first + at.start, 16), 16), :]

    def rxa_parts(o, first):
        return [from_x(rxa.at[k - 1, o], first) for k in range(1, xs)]

    def rxb_parts(first):
        return [from_x(rxb.at[k - 1], first) for k in range(1, xs)]

    def step(t, carry):
        for unit in units:
            for d in (0, 1):
                s = z - t if d == 1 else z + t

                @pl.when((s >= 0) & (s < zs))
                def _():
                    gather_z(d, s, unit).wait_recv()

                    @pl.when(has_next(d))
                    def _():
                        gather_z(d, s, unit).start()
                    if unit is None:
                        for k in range(1, xs):
                            gather_xa(k, s, x).start()

        def slab(j, c):
            far = jnp.where(z < zs // 2, 1, -1)
            s = jnp.where(j == 0, z - far * (t - 1), z + far * t)

            @pl.when((s >= 0) & (s < zs) & (j + t >= 2))
            def _():
                compute(s)
            return c

        lax.fori_loop(0, 2, slab, 0)

        for piece in [q for sx in range(xs) for q in b_pieces(sx)] + a_pieces():
            def flow(j, c):
                d = jnp.where(z < zs // 2, 1 - j, j)
                o = jnp.where(d == 0, zs - 1 - t, t)
                dist = jnp.where(d == 0, z - o, o - z)
                fed = jnp.where(d == 0, zs - 1 - z, z)

                @pl.when(dist > 0)
                def _():
                    parts = []
                    if piece[0] is None:
                        if piece[1] == 0:
                            for k in range(1, xs):
                                reduce_xa(k, o).wait_recv()
                        parts = rxa_parts(o, piece[1])

                    @pl.when(fed > 0)
                    def _():
                        reduce_z(d, o, piece).wait_recv()
                    read, write = p_part(o, piece)
                    add_rows(piece[2], write, [read, rz_part(d, o, piece)] + parts)
                    reduce_z(d, o, piece).start()
                return c

            lax.fori_loop(0, 2, flow, 0)
        return carry

    lax.fori_loop(1, zs, step, 0)

    def take(piece):
        for d in (0, 1):
            @pl.when(has_next(1 - d))
            def _():
                reduce_z(d, z, piece).wait_recv()

    for k in range(1, xs):
        for piece in b_pieces(other(k)):
            take(piece)
            read, write = p_part(z, piece)
            add_rows(piece[2], write, [read, rz_part(0, z, piece), rz_part(1, z, piece)])
        reduce_xb(k).start()

    def out_at(base):
        def write(i, value):
            out_ref[pl.ds(pl.multiple_of(base + i, 16), 16), :] = value.astype(out_ref.dtype)
        return write

    for k in range(1, xs):
        reduce_xa(k, z).wait_recv()
    for piece in a_pieces():
        take(piece)
        add_rows(
            piece[2], out_at(piece[1]),
            [p_part(z, piece)[0], rz_part(0, z, piece), rz_part(1, z, piece)]
            + rxa_parts(z, piece[1]),
        )
    for k in range(1, xs):
        reduce_xb(k).wait_recv()
    for piece in b_pieces(x):
        take(piece)
        add_rows(
            piece[2], out_at(ra + piece[1]),
            [p_part(z, piece)[0], rz_part(0, z, piece), rz_part(1, z, piece)]
            + rxb_parts(piece[1]),
        )

    for k in range(1, xs):
        gather_xb(k, x).wait_send()
        reduce_xb(k).wait_send()

    def sent(s, carry):
        for k in range(1, xs):
            gather_xa(k, s, x).wait_send()
            reduce_xa(k, s).wait_send()
        for d in (0, 1):
            behind = s <= z if d == 1 else s >= z
            ahead = s > z if d == 1 else s < z

            @pl.when(has_next(d) & behind)
            def _():
                for unit in units:
                    gather_z(d, s, unit).wait_send()

            @pl.when(ahead)
            def _():
                for piece in a_pieces() + [q for sx in range(xs) for q in b_pieces(sx)]:
                    reduce_z(d, s, piece).wait_send()
        return carry

    lax.fori_loop(0, zs, sent, 0)


def expert_sum(slot_rows, gate_weight, up_weight, down_weight, tensor):
    rows, width = slot_rows.shape
    hidden = gate_weight.shape[0]
    zs = ROWS_Z if tensor % ROWS_Z == 0 else 1
    xs = tensor // zs
    ra = rows * 5 // 8 // 16 * 16
    rb = rows - ra
    wide = 512 if width % 512 == 0 else 128
    dt = slot_rows.dtype
    dma = pltpu.SemaphoreType.DMA
    pieces = len(cuts(ra)) + xs * len(cuts(rb))
    flops = 6 * rows * tensor * width * hidden
    return pl.pallas_call(
        functools.partial(expert_kernel, zs, xs, ra, wide),
        out_shape=jax.ShapeDtypeStruct((rows, width), dt),
        in_specs=[pl.BlockSpec(memory_space=pltpu.VMEM)]
        + [pl.BlockSpec(memory_space=pl.ANY)] * 3,
        out_specs=pl.BlockSpec(memory_space=pltpu.VMEM),
        scratch_shapes=[
            pltpu.VMEM((zs, xs * rows, width), dt),
            pltpu.VMEM((zs, xs * rows, width), dt),
            pltpu.VMEM((2, zs, ra + xs * rb, width), dt),
            pltpu.VMEM((xs - 1, zs, ra, width), dt),
            pltpu.VMEM((xs - 1, rb, width), dt),
            pltpu.VMEM((xs * rows, hidden), dt),
            pltpu.VMEM(gate_weight.shape, dt),
            pltpu.VMEM(up_weight.shape, dt),
            pltpu.VMEM(down_weight.shape, dt),
            dma((3,)),
            dma((2, zs, xs + 1)), dma((zs, xs + 1)),
            dma((zs, xs - 1)), dma((zs, xs - 1)),
            dma((xs - 1,)), dma((xs - 1,)),
            dma((2, zs, pieces)), dma((2, zs, pieces)),
            dma((zs, xs - 1)), dma((zs, xs - 1)),
            dma((xs - 1,)), dma((xs - 1,)),
        ],
        compiler_params=pltpu.CompilerParams(
            collective_id=0, has_side_effects=True, vmem_limit_bytes=60 * 2**20
        ),
        cost_estimate=pl.CostEstimate(
            flops=flops, bytes_accessed=6 * width * hidden + 4 * rows * width,
            transcendentals=rows * tensor * hidden,
        ),
    )(slot_rows, gate_weight, up_weight, down_weight)


def on_device(tensor, tokens, expert_ids, gate_probs, gate_weight, up_weight, down_weight):
    count, width = tokens.shape
    spans = count // CT
    is_window = expert_ids == 0
    routed = jnp.any(is_window, axis=1)
    gate_share = jnp.sum(jnp.where(is_window, gate_probs, 0.0), axis=1)
    routed_blocks = routed.reshape(spans, CT)
    slot_place = jnp.cumsum(routed_blocks.astype(jnp.int32), axis=1) - 1
    selector = (
        (slot_place[:, None, :] == jnp.arange(CAP, dtype=jnp.int32)[None, :, None])
        & routed_blocks[:, None, :]
    ).astype(jnp.bfloat16)
    slot_rows = jnp.einsum(
        "bst,btd->bsd", selector, tokens.reshape(spans, CT, width),
        preferred_element_type=jnp.float32,
    ).astype(jnp.bfloat16)
    expert_out = expert_sum(
        slot_rows.reshape(spans * CAP, width), gate_weight.T, up_weight.T, down_weight, tensor
    )
    picked = jnp.einsum(
        "bst,bsd->btd", selector, expert_out.reshape(spans, CAP, width),
        preferred_element_type=jnp.float32,
    )
    mixed = gate_share.reshape(spans, CT)[:, :, None] * picked
    return mixed.astype(jnp.bfloat16).reshape(count, width)


def solution(mesh):
    in_specs = (
        P(("dp", "tensor"), None),
        P(("dp", "tensor"), None),
        P(("dp", "tensor"), None),
        P(None, "tensor"),
        P(None, "tensor"),
        P("tensor", None),
    )
    out_specs = P(("dp", "tensor"), None)
    return jax.shard_map(
        functools.partial(on_device, mesh.shape["tensor"]),
        mesh=mesh, in_specs=in_specs, out_specs=out_specs, check_vma=False,
    )
```

```python
import functools

import jax
import jax.numpy as jnp
from jax import lax
from jax.experimental import pallas as pl
from jax.experimental.pallas import tpu as pltpu
from jax.sharding import PartitionSpec as P

CT = 128
CAP = 32
ROWS_Z = 4
PIECE = 80
MESH = pl.DeviceIdType.MESH


def cuts(rows):
    return [(at, min(PIECE, rows - at)) for at in range(0, rows, PIECE)]


def dot_t(a, b):
    return lax.dot_general(
        a, b, (((1,), (1,)), ((), ())), preferred_element_type=jnp.float32
    )


def expert_kernel(
    zs, xs, ra, wide,
    slot_ref, gw_hbm, uw_hbm, dw_hbm, out_ref,
    g, p, rz, rxa, rxb, h, gw, uw, dw,
    wsem, agz_s, agz_r, axa_s, axa_r, axb_s, axb_r,
    rz_s, rz_r, rxa_s, rxa_r, rxb_s, rxb_r,
):
    rows, width = slot_ref.shape
    rb = rows - ra
    hidden = gw.shape[0]
    me = lax.axis_index("tensor")
    dp = lax.axis_index("dp")
    z = me // xs
    x = me % xs

    def dev(zz, xx):
        return (dp, zz * xs + xx)

    def a_rows(sx):
        return pl.ds(pl.multiple_of(sx * rows, 16), ra)

    def b_rows(sx):
        return pl.ds(pl.multiple_of(sx * rows + ra, 16), rb)

    def other(k):
        return (x + k) % xs

    def source(k):
        return (x + xs - k) % xs

    def unit_rows(unit):
        return a_rows(x) if unit is None else b_rows(unit)

    def unit_sem(unit):
        return 0 if unit is None else 1 + unit

    a_cuts = cuts(ra)
    b_cuts = cuts(rb)

    def a_pieces():
        return [(None, at, n, i) for i, (at, n) in enumerate(a_cuts)]

    def b_pieces(sx):
        return [
            (sx, at, n, len(a_cuts) + sx * len(b_cuts) + i)
            for i, (at, n) in enumerate(b_cuts)
        ]

    def p_base(piece):
        sx, at = piece[:2]
        return x * rows + at if sx is None else sx * rows + ra + at

    def rz_base(piece):
        sx, at = piece[:2]
        return at if sx is None else ra + sx * rb + at

    units = [None] + list(range(xs))

    def copy(src, dst, s, r, to):
        return pltpu.make_async_remote_copy(
            src_ref=src, dst_ref=dst, send_sem=s, recv_sem=r,
            device_id=to, device_id_type=MESH,
        )

    def gather_z(d, s, unit):
        part = g.at[s, unit_rows(unit)]
        i = unit_sem(unit)
        return copy(part, part, agz_s.at[d, s, i], agz_r.at[s, i], dev(z + 2 * d - 1, x))

    def gather_xa(k, s, sx):
        part = g.at[s, a_rows(sx)]
        return copy(part, part, axa_s.at[s, k - 1], axa_r.at[s, k - 1], dev(z, other(k)))

    def gather_xb(k, sx):
        part = g.at[z, b_rows(sx)]
        return copy(part, part, axb_s.at[k - 1], axb_r.at[k - 1], dev(z, other(k)))

    def reduce_xa(k, s):
        return copy(
            p.at[s, a_rows(other(k))], rxa.at[k - 1, s],
            rxa_s.at[s, k - 1], rxa_r.at[s, k - 1], dev(z, other(k)),
        )

    def reduce_xb(k):
        return copy(
            p.at[z, b_rows(other(k))], rxb.at[k - 1],
            rxb_s.at[k - 1], rxb_r.at[k - 1], dev(z, other(k)),
        )

    def reduce_z(d, o, piece):
        n, i = piece[2:]
        return copy(
            p.at[o, pl.ds(pl.multiple_of(p_base(piece), 16), n)],
            rz.at[d, o, pl.ds(pl.multiple_of(rz_base(piece), 16), n)],
            rz_s.at[d, o, i], rz_r.at[d, o, i], dev(z + 2 * d - 1, x),
        )

    def has_next(d):
        return z < zs - 1 if d == 1 else z > 0

    weights = [
        pltpu.make_async_copy(a, b, wsem.at[i])
        for i, (a, b) in enumerate(((gw_hbm, gw), (uw_hbm, uw), (dw_hbm, dw)))
    ]
    for w in weights:
        w.start()

    barrier = pltpu.get_barrier_semaphore()
    for d in (0, 1):
        @pl.when(has_next(d))
        def _():
            pl.semaphore_signal(barrier, inc=1, device_id=dev(z + 2 * d - 1, x), device_id_type=MESH)
    for k in range(1, xs):
        pl.semaphore_signal(barrier, inc=1, device_id=dev(z, other(k)), device_id_type=MESH)
    g[z, pl.ds(pl.multiple_of(x * rows, 16), rows), :] = slot_ref[...]
    ends = (z == 0).astype(jnp.int32) + (z == zs - 1).astype(jnp.int32)
    pl.semaphore_wait(barrier, xs + 1 - ends)

    for k in range(1, xs):
        gather_xb(k, x).start()
    for d in (0, 1):
        @pl.when(has_next(d))
        def _():
            gather_z(d, z, None).start()
            gather_z(d, z, x).start()
    for k in range(1, xs):
        gather_xa(k, z, x).start()

    @pl.when(z == zs - 1)
    def _():
        rz[0] = jnp.zeros(rz.shape[1:], rz.dtype)

    @pl.when(z == 0)
    def _():
        rz[1] = jnp.zeros(rz.shape[1:], rz.dtype)

    for k in range(1, xs):
        gather_xb(k, source(k)).wait_recv()
        for d in (0, 1):
            @pl.when(has_next(d))
            def _():
                gather_z(d, z, source(k)).start()

    def compute(s):
        for k in range(1, xs):
            gather_xa(k, s, source(k)).wait_recv()
        for c in range(0, hidden, 256):
            n = min(256, hidden - c)
            lhs = g[s]
            gate = dot_t(lhs, gw[c:c + n, :])
            up = dot_t(lhs, uw[c:c + n, :])
            h[:, c:c + n] = (gate / (1.0 + jnp.exp(-gate)) * up).astype(h.dtype)

        def columns(i, carry):
            at = pl.ds(pl.multiple_of(i * wide, 128), wide)
            p[s, :, at] = jnp.dot(
                h[...], dw[:, at], preferred_element_type=jnp.float32
            ).astype(p.dtype)
            return carry

        lax.fori_loop(0, width // wide, columns, 0)
        for k in range(1, xs):
            reduce_xa(k, s).start()

    for w in weights:
        w.wait()
    compute(z)

    def add_rows(count, target, parts):
        def body(i, carry):
            i = pl.multiple_of(i * 16, 16)
            total = None
            for part in parts:
                value = part(pl.ds(i, 16)).astype(jnp.float32)
                total = value if total is None else total + value
            target(i, total)
            return carry

        lax.fori_loop(0, count // 16, body, 0)

    def p_part(o, piece):
        base = p_base(piece)

        def read(at):
            return p[o, pl.ds(pl.multiple_of(base + at.start, 16), 16), :]

        def write(i, value):
            p[o, pl.ds(pl.multiple_of(base + i, 16), 16), :] = value.astype(p.dtype)

        return read, write

    def rz_part(d, o, piece):
        base = rz_base(piece)

        def read(at):
            return rz[d, o, pl.ds(pl.multiple_of(base + at.start, 16), 16), :]

        return read

    def from_x(ref, first):
        return lambda at: ref[pl.ds(pl.multiple_of(first + at.start, 16), 16), :]

    def rxa_parts(o, first):
        return [from_x(rxa.at[k - 1, o], first) for k in range(1, xs)]

    def rxb_parts(first):
        return [from_x(rxb.at[k - 1], first) for k in range(1, xs)]

    def step(t, carry):
        for unit in units:
            for d in (0, 1):
                s = z - t if d == 1 else z + t

                @pl.when((s >= 0) & (s < zs))
                def _():
                    gather_z(d, s, unit).wait_recv()

                    @pl.when(has_next(d))
                    def _():
                        gather_z(d, s, unit).start()
                    if unit is None:
                        for k in range(1, xs):
                            gather_xa(k, s, x).start()

        def slab(j, c):
            far = jnp.where(z < zs // 2, 1, -1)
            s = jnp.where(j == 0, z - far * (t - 1), z + far * t)

            @pl.when((s >= 0) & (s < zs) & (j + t >= 2))
            def _():
                compute(s)
            return c

        lax.fori_loop(0, 2, slab, 0)

        for piece in [q for sx in range(xs) for q in b_pieces(sx)] + a_pieces():
            def flow(j, c):
                d = jnp.where(z < zs // 2, 1 - j, j)
                o = jnp.where(d == 0, zs - 1 - t, t)
                dist = jnp.where(d == 0, z - o, o - z)
                fed = jnp.where(d == 0, zs - 1 - z, z)

                @pl.when(dist > 0)
                def _():
                    parts = []
                    if piece[0] is None:
                        if piece[1] == 0:
                            for k in range(1, xs):
                                reduce_xa(k, o).wait_recv()
                        parts = rxa_parts(o, piece[1])

                    @pl.when(fed > 0)
                    def _():
                        reduce_z(d, o, piece).wait_recv()
                    read, write = p_part(o, piece)
                    add_rows(piece[2], write, [read, rz_part(d, o, piece)] + parts)
                    reduce_z(d, o, piece).start()
                return c

            lax.fori_loop(0, 2, flow, 0)
        return carry

    lax.fori_loop(1, zs, step, 0)

    def take(piece):
        for d in (0, 1):
            @pl.when(has_next(1 - d))
            def _():
                reduce_z(d, z, piece).wait_recv()

    for k in range(1, xs):
        for piece in b_pieces(other(k)):
            take(piece)
            read, write = p_part(z, piece)
            add_rows(piece[2], write, [read, rz_part(0, z, piece), rz_part(1, z, piece)])
        reduce_xb(k).start()

    def out_at(base):
        def write(i, value):
            out_ref[pl.ds(pl.multiple_of(base + i, 16), 16), :] = value.astype(out_ref.dtype)
        return write

    for k in range(1, xs):
        reduce_xa(k, z).wait_recv()
    for piece in a_pieces():
        take(piece)
        add_rows(
            piece[2], out_at(piece[1]),
            [p_part(z, piece)[0], rz_part(0, z, piece), rz_part(1, z, piece)]
            + rxa_parts(z, piece[1]),
        )
    for k in range(1, xs):
        reduce_xb(k).wait_recv()
    for piece in b_pieces(x):
        take(piece)
        add_rows(
            piece[2], out_at(ra + piece[1]),
            [p_part(z, piece)[0], rz_part(0, z, piece), rz_part(1, z, piece)]
            + rxb_parts(piece[1]),
        )

    for k in range(1, xs):
        gather_xb(k, x).wait_send()
        reduce_xb(k).wait_send()

    def sent(s, carry):
        for k in range(1, xs):
            gather_xa(k, s, x).wait_send()
            reduce_xa(k, s).wait_send()
        for d in (0, 1):
            behind = s <= z if d == 1 else s >= z
            ahead = s > z if d == 1 else s < z

            @pl.when(has_next(d) & behind)
            def _():
                for unit in units:
                    gather_z(d, s, unit).wait_send()

            @pl.when(ahead)
            def _():
                for piece in a_pieces() + [q for sx in range(xs) for q in b_pieces(sx)]:
                    reduce_z(d, s, piece).wait_send()
        return carry

    lax.fori_loop(0, zs, sent, 0)


def expert_sum(slot_rows, gate_weight, up_weight, down_weight, tensor):
    rows, width = slot_rows.shape
    hidden = gate_weight.shape[0]
    zs = ROWS_Z if tensor % ROWS_Z == 0 else 1
    xs = tensor // zs
    ra = rows * 5 // 8 // 16 * 16
    rb = rows - ra
    wide = 512 if width % 512 == 0 else 128
    dt = slot_rows.dtype
    dma = pltpu.SemaphoreType.DMA
    pieces = len(cuts(ra)) + xs * len(cuts(rb))
    flops = 6 * rows * tensor * width * hidden
    return pl.pallas_call(
        functools.partial(expert_kernel, zs, xs, ra, wide),
        out_shape=jax.ShapeDtypeStruct((rows, width), dt),
        in_specs=[pl.BlockSpec(memory_space=pltpu.VMEM)]
        + [pl.BlockSpec(memory_space=pl.ANY)] * 3,
        out_specs=pl.BlockSpec(memory_space=pltpu.VMEM),
        scratch_shapes=[
            pltpu.VMEM((zs, xs * rows, width), dt),
            pltpu.VMEM((zs, xs * rows, width), dt),
            pltpu.VMEM((2, zs, ra + xs * rb, width), dt),
            pltpu.VMEM((xs - 1, zs, ra, width), dt),
            pltpu.VMEM((xs - 1, rb, width), dt),
            pltpu.VMEM((xs * rows, hidden), dt),
            pltpu.VMEM(gate_weight.shape, dt),
            pltpu.VMEM(up_weight.shape, dt),
            pltpu.VMEM(down_weight.shape, dt),
            dma((3,)),
            dma((2, zs, xs + 1)), dma((zs, xs + 1)),
            dma((zs, xs - 1)), dma((zs, xs - 1)),
            dma((xs - 1,)), dma((xs - 1,)),
            dma((2, zs, pieces)), dma((2, zs, pieces)),
            dma((zs, xs - 1)), dma((zs, xs - 1)),
            dma((xs - 1,)), dma((xs - 1,)),
        ],
        compiler_params=pltpu.CompilerParams(
            collective_id=0, has_side_effects=True, vmem_limit_bytes=60 * 2**20
        ),
        cost_estimate=pl.CostEstimate(
            flops=flops, bytes_accessed=6 * width * hidden + 4 * rows * width,
            transcendentals=rows * tensor * hidden,
        ),
    )(slot_rows, gate_weight, up_weight, down_weight)


def on_device(tensor, tokens, expert_ids, gate_probs, gate_weight, up_weight, down_weight):
    count, width = tokens.shape
    spans = count // CT
    is_window = expert_ids == 0
    routed = jnp.any(is_window, axis=1)
    gate_share = jnp.sum(jnp.where(is_window, gate_probs, 0.0), axis=1)
    routed_blocks = routed.reshape(spans, CT)
    slot_place = jnp.cumsum(routed_blocks.astype(jnp.int32), axis=1) - 1
    selector = (
        (slot_place[:, None, :] == jnp.arange(CAP, dtype=jnp.int32)[None, :, None])
        & routed_blocks[:, None, :]
    ).astype(jnp.bfloat16)
    slot_rows = jnp.einsum(
        "bst,btd->bsd", selector, tokens.reshape(spans, CT, width),
        preferred_element_type=jnp.float32,
    ).astype(jnp.bfloat16)
    expert_out = expert_sum(
        slot_rows.reshape(spans * CAP, width), gate_weight.T, up_weight.T, down_weight, tensor
    )
    picked = jnp.einsum(
        "bst,bsd->btd", selector, expert_out.reshape(spans, CAP, width),
        preferred_element_type=jnp.float32,
    )
    mixed = gate_share.reshape(spans, CT)[:, :, None] * picked
    return mixed.astype(jnp.bfloat16).reshape(count, width)


def solution(mesh):
    in_specs = (
        P(("dp", "tensor"), None),
        P(("dp", "tensor"), None),
        P(("dp", "tensor"), None),
        P(None, "tensor"),
        P(None, "tensor"),
        P("tensor", None),
    )
    out_specs = P(("dp", "tensor"), None)
    return jax.shard_map(
        functools.partial(on_device, mesh.shape["tensor"]),
        mesh=mesh, in_specs=in_specs, out_specs=out_specs, check_vma=False,
    )
```
